256 devices in a mesh: row: 16 (over x_lo, z), col: 16 (over y, x_hi, core).
Axes of the slice: x: 4 (x_hi: 2, x_lo: 2; x = x_hi * 2 + x_lo), y: 4, z: 8, core: 2. Of those that a mesh axis runs over, the one named last changes fastest.
Arguments:
- pair_input: float32 [512, 512, 128], P('row', 'col'), may hold values from -6 to 6
- outgoing_in: bfloat16 [128, 640], replicated, may hold values from -0.5 to 0.5
- outgoing_out: bfloat16 [128, 128], replicated, may hold values from -0.5 to 0.5
- incoming_in: bfloat16 [128, 640], replicated, may hold values from -0.5 to 0.5
- incoming_out: bfloat16 [128, 128], replicated, may hold values from -0.5 to 0.5
Outputs:
- pair_output: float32 [512, 512, 128], P('row', 'col')
The draws below stay inside these ranges and needn't reach their ends.
All inputs are finite; a program needn't handle non-finite values.
Results may differ from the reference program's by a relative error of at most 0.011.
Values may be sent and summed in bfloat16 or wider, within the bound.
A program may use at most 128 MiB of HBM per device.

```python
import jax
import jax.numpy as jnp
from jax import lax

C = 128
CH = 128
N = 512


def level_of(key, extent, split, low, top_value):
    def one(position, parts):
        draws = jax.random.uniform(jax.random.fold_in(jax.random.fold_in(key, 6), position), (parts,), jnp.float32, low / len(split), top_value / len(split))
        return jnp.repeat(jnp.exp(draws), extent[position] // parts).reshape((-1,) + (1,) * (len(extent) - position - 1))

    loudness = one(*split[0])
    for cut in split[1:]:
        loudness = loudness * one(*cut)
    return loudness


def scatter_about(own_key, dims, deviation, limit, shards=(), held_as=jnp.bfloat16):
    gain = level_of(own_key, dims, shards, -0.22, 0.18) if shards else 1.0
    array = jax.random.normal(own_key, dims, jnp.float32) * deviation * gain
    return jnp.minimum(jnp.maximum(array, -limit), limit).astype(held_as)


def setup_inputs(seed: int = 0) -> dict:
    splits = jax.random.split(jax.random.key(seed), 6)
    return {
        "pair_input": scatter_about(splits[0], (N, N, C), 1.0, 6.0, ((0, 16), (1, 16)), jnp.float32),
        "outgoing_in": scatter_about(splits[1], (C, 4 * CH + C), C ** -0.5, 0.5),
        "outgoing_out": scatter_about(splits[2], (CH, C), CH ** -0.5, 0.5),
        "incoming_in": scatter_about(splits[3], (C, 4 * CH + C), C ** -0.5, 0.5),
        "incoming_out": scatter_about(splits[4], (CH, C), CH ** -0.5, 0.5),
    }


def normalize(v):
    mean = lax.optimization_barrier(jnp.mean(v, axis=-1, keepdims=True))
    cent = v - mean
    var = lax.optimization_barrier(jnp.mean(cent * cent, axis=-1, keepdims=True))
    return cent * lax.rsqrt(var + 1e-05)

def triangle(pair, w_in, w_out, outgoing):
    normed = normalize(pair).astype(jnp.bfloat16)
    proj = jnp.dot(normed.reshape(-1, C), w_in, preferred_element_type=jnp.float32).reshape(N, N, 4 * CH + C)
    left = (jax.nn.sigmoid(proj[..., :CH]) * proj[..., CH:2 * CH]).astype(jnp.bfloat16)
    right = (jax.nn.sigmoid(proj[..., 2 * CH:3 * CH]) * proj[..., 3 * CH:4 * CH]).astype(jnp.bfloat16)
    gate = jax.nn.sigmoid(proj[..., 4 * CH:])
    left_f = left.astype(jnp.float32)
    right_f = right.astype(jnp.float32)
    if outgoing:
        tri = jnp.einsum('ikc,jkc->ijc', left_f, right_f, precision=lax.Precision.HIGHEST)
    else:
        tri = jnp.einsum('kic,kjc->ijc', left_f, right_f, precision=lax.Precision.HIGHEST)
    tnorm = normalize(tri).astype(jnp.bfloat16)
    update = jnp.dot(tnorm.reshape(-1, CH), w_out, preferred_element_type=jnp.float32).reshape(N, N, C)
    return pair + gate * update

def reference(pair_input, outgoing_in, outgoing_out, incoming_in, incoming_out):
    middle = triangle(pair_input, outgoing_in, outgoing_out, True)
    return triangle(middle, incoming_in, incoming_out, False)
```

```python
import functools

import jax
import jax.numpy as jnp
from jax import lax
from jax.experimental import pallas as pl
from jax.experimental.pallas import tpu as pltpu
from jax.sharding import PartitionSpec as P

MESH = pl.DeviceIdType.MESH
F32 = jnp.float32
BF16 = jnp.bfloat16
EPS = 1e-05


def sigmoid(v):
    return 0.5 * jnp.tanh(0.5 * v) + 0.5


def device(x, y, z, core):
    return (x % 2 * 8 + z, y * 4 + x // 2 * 2 + core)


def regroup(tiles):
    lane = lax.broadcasted_iota(jnp.int32, tiles[0].shape, 1)
    low = lane < 64
    even = lane // 32 % 2 == 0
    t = list(tiles)
    for a, b in ((0, 2), (1, 3)):
        t[a], t[b] = (
            jnp.where(low, t[a], pltpu.roll(t[b], 64, 1)),
            jnp.where(low, pltpu.roll(t[a], 64, 1), t[b]),
        )
    for a, b in ((0, 1), (2, 3)):
        t[a], t[b] = (
            jnp.where(even, t[a], pltpu.roll(t[b], 32, 1)),
            jnp.where(even, pltpu.roll(t[a], 96, 1), t[b]),
        )
    return t


def kernel(
    z_ref, w1_ref, u1_ref, w2_ref, u2_ref, out_ref,
    pair, normed, gate, wt, ut, stage, stage2,
    send, recv, lmat, rmat, tsend, trecv,
    send_sem, recv_sem, ex_send, ex_recv, tsend_sem, trecv_sem, plane_sem,
):
    row, col = lax.axis_index("row"), lax.axis_index("col")
    z = row % 8
    y = col // 4
    x = col // 2 % 2 * 2 + row // 8
    core = col % 2
    me = x * 32 + y * 8 + z

    barrier = pltpu.get_barrier_semaphore()

    def plane(o):
        return device((x + o // 4) % 4, (y + o % 4) % 4, z, core)

    def greet_ring(o, _):
        pl.semaphore_signal(barrier, inc=1, device_id=device(x, y, (z + o) % 8, core), device_id_type=MESH)
        return 0

    def greet_plane(o, _):
        pl.semaphore_signal(barrier, inc=1, device_id=plane(o), device_id_type=MESH)
        return 0

    def greet_again(o, _):
        pl.semaphore_signal(plane_sem, inc=1, device_id=plane(o), device_id_type=MESH)
        return 0

    lax.fori_loop(1, 8, greet_ring, 0)
    lax.fori_loop(1, 16, greet_plane, 0)
    pl.semaphore_signal(barrier, inc=1, device_id=device(x, y, z, 1 - core), device_id_type=MESH)

    for k, (w_ref, u_ref) in enumerate(((w1_ref, u1_ref), (w2_ref, u2_ref))):
        for b in range(5):
            wt[k, b] = w_ref[:, 128 * b : 128 * b + 128].astype(F32).T.astype(BF16)
        ut[k] = u_ref[...].astype(F32).T.astype(BF16)

    for a in range(8):
        rows = z_ref[:, a].reshape(128, 128)
        pair[:, 128 * a : 128 * a + 128] = rows.T

    pl.semaphore_wait(barrier, 23)
    lax.fori_loop(1, 16, greet_again, 0)

    def norm_pair():
        v = pair[...]
        cent = v - jnp.mean(v, axis=0, keepdims=True)
        var = jnp.mean(cent * cent, axis=0, keepdims=True)
        normed[...] = (cent * lax.rsqrt(var + EPS)).astype(BF16)

    def update(k, outgoing):
        norm_pair()
        zn = normed[...]
        if k == 0:
            pl.semaphore_wait(plane_sem, 15)

        for dx in range(4):
            xd = (x + dx) % 4
            w = wt[k, :4, pl.ds(pl.multiple_of(xd * 32, 32), 32), :].reshape(128, 128)
            p = jnp.dot(w, zn, preferred_element_type=F32)
            left = sigmoid(p[0:32]) * p[32:64]
            right = sigmoid(p[64:96]) * p[96:128]
            for a in range(8):
                stage[pl.ds(a, 32, stride=16), :] = left[:, 128 * a : 128 * a + 128]
                stage[pl.ds(8 + a, 32, stride=16), :] = right[:, 128 * a : 128 * a + 128]
            send[k, xd] = stage[...].reshape(32, 16, 128).astype(BF16)

            def push(o, _, dx=dx, xd=xd):
                yd, zd = (y + o // 8) % 4, (z + o) % 8
                pltpu.make_async_remote_copy(
                    src_ref=send.at[k, xd, yd * 8 + zd],
                    dst_ref=recv.at[k, x, y * 8 + z],
                    send_sem=send_sem.at[k, dx],
                    recv_sem=recv_sem.at[k, dx],
                    device_id=device(xd, yd, zd, core),
                    device_id_type=MESH,
                ).start()
                return 0

            if dx == 0:
                recv[k, x, y * 8 + z] = send[k, x, y * 8 + z]
            lax.fori_loop(1 if dx == 0 else 0, 32, push, 0)

        gate[...] = sigmoid(jnp.dot(wt[k, 4], zn, preferred_element_type=F32))

        exchanges = []
        for dx in range(4):
            xs = (x + 4 - dx) % 4
            part = recv.at[k, xs, pl.ds(0, 31)] if dx == 0 else recv.at[k, xs]
            pltpu.make_async_copy(part, part, recv_sem.at[k, dx]).wait()
            kc = xs // 2 * 2 + core
            for zs in range(8):
                tiles = [recv[k, xs, ys * 8 + zs].astype(F32) for ys in range(4)]
                t = regroup(tiles)
                base = zs // 2 * 32
                for h in range(2):
                    pair_l = jnp.concatenate([t[2 * h][0:8], t[2 * h + 1][0:8]], axis=0)
                    pair_r = jnp.concatenate([t[2 * h][8:16], t[2 * h + 1][8:16]], axis=0)
                    here = pl.ds(base + 16 * h, 16)
                    lmat[k, kc, xs % 2, zs % 2, here, :] = pair_l.astype(BF16)
                    rmat[k, kc, xs % 2, zs % 2, here, :] = pair_r.astype(BF16)

            def swap(ref, n):
                copy = pltpu.make_async_remote_copy(
                    src_ref=ref,
                    dst_ref=ref,
                    send_sem=ex_send.at[k, dx, n],
                    recv_sem=ex_recv.at[k, dx, n],
                    device_id=device(x, y, z, 1 - core),
                    device_id_type=MESH,
                )
                copy.start()
                exchanges.append(copy)

            swap(lmat.at[k, kc, xs % 2], 0)
            if outgoing:
                swap(rmat.at[k, kc, xs % 2, 1 - core], 1)
        for copy in exchanges:
            copy.wait()

        if outgoing:
            a = jnp.concatenate([lmat[k, kc].reshape(512, 128) for kc in range(4)], axis=1)
            b = jnp.concatenate([rmat[k, kc, :, core].reshape(256, 128) for kc in range(4)], axis=1)
            tri = lax.dot_general(a, b, (((1,), (1,)), ((), ())), preferred_element_type=F32)
        else:
            a = jnp.concatenate([lmat[k, kc].reshape(512, 128) for kc in range(4)], axis=1)
            b = jnp.concatenate([rmat[k, 2 * xh + core].reshape(512, 128) for xh in range(2)], axis=1)
            tri = lax.dot_general(a, b, (((0,), (0,)), ((), ())), preferred_element_type=F32)
        for m in range(16):
            if outgoing:
                r = m // 8 * 8 + m % 4 * 2 + m // 4 % 2
            else:
                r = m % 4 * 4 + m // 4
            for n in range(2):
                tiles = [
                    tri[32 * m + 8 * u : 32 * m + 8 * u + 8, 128 * n : 128 * n + 128]
                    for u in range(4)
                ]
                for t, tile in enumerate(regroup(tiles)):
                    tsend[k, r, 4 * n + t if outgoing else 2 * t + n] = tile.astype(BF16)

        def give(o, _):
            xd, yd, zd = (x + o // 32) % 4, (y + o // 8 % 4) % 4, (z + o) % 8
            pltpu.make_async_remote_copy(
                src_ref=tsend.at[k, xd % 2 * 8 + zd, yd * 2 + xd // 2],
                dst_ref=trecv.at[k, me],
                send_sem=tsend_sem.at[k],
                recv_sem=trecv_sem.at[k],
                device_id=device(xd, yd, zd, core),
                device_id_type=MESH,
            ).start()
            return 0

        lax.fori_loop(1, 128, give, 0)
        trecv[k, me] = tsend[k, x % 2 * 8 + z, y * 2 + x // 2]
        part = trecv.at[k, pl.ds(0, 127)]
        pltpu.make_async_copy(part, part, trecv_sem.at[k]).wait()

        v = trecv[k].astype(F32)
        cent = v - jnp.mean(v, axis=0, keepdims=True)
        var = jnp.mean(cent * cent, axis=0, keepdims=True)
        stage2[...] = (cent * lax.rsqrt(var + EPS)).reshape(1024, 128)
        tn = jnp.concatenate(
            [stage2[pl.ds(a, 128, stride=8), :].astype(BF16) for a in range(8)], axis=1
        )
        change = jnp.dot(ut[k], tn, preferred_element_type=F32)
        pair[...] = pair[...] + gate[...] * change

    update(0, True)
    update(1, False)

    for a in range(8):
        out_ref[:, a] = pair[:, 128 * a : 128 * a + 128].T.reshape(4, 32, 128)

    for k in range(2):
        for dx in range(4):
            part = send.at[k, 0, pl.ds(0, 31)] if dx == 0 else send.at[k, 0]
            pltpu.make_async_copy(part, part, send_sem.at[k, dx]).wait()
        part = trecv.at[k, pl.ds(0, 127)]
        pltpu.make_async_copy(part, part, tsend_sem.at[k]).wait()


def per_device(pair_input, outgoing_in, outgoing_out, incoming_in, incoming_out):
    vmem = pl.BlockSpec(memory_space=pltpu.VMEM)
    out = pl.pallas_call(
        kernel,
        out_shape=jax.ShapeDtypeStruct((4, 8, 32, 128), F32),
        in_specs=[vmem] * 5,
        out_specs=vmem,
        scratch_shapes=[
            pltpu.VMEM((128, 1024), F32),
            pltpu.VMEM((128, 1024), BF16),
            pltpu.VMEM((128, 1024), F32),
            pltpu.VMEM((2, 5, 128, 128), BF16),
            pltpu.VMEM((2, 128, 128), BF16),
            pltpu.VMEM((512, 128), F32),
            pltpu.VMEM((1024, 128), F32),
            pltpu.VMEM((2, 4, 32, 16, 128), BF16),
            pltpu.VMEM((2, 4, 32, 16, 128), BF16),
            pltpu.VMEM((2, 4, 2, 2, 128, 128), BF16),
            pltpu.VMEM((2, 4, 2, 2, 128, 128), BF16),
            pltpu.VMEM((2, 16, 8, 8, 128), BF16),
            pltpu.VMEM((2, 128, 8, 128), BF16),
            pltpu.SemaphoreType.DMA((2, 4)),
            pltpu.SemaphoreType.DMA((2, 4)),
            pltpu.SemaphoreType.DMA((2, 4, 2)),
            pltpu.SemaphoreType.DMA((2, 4, 2)),
            pltpu.SemaphoreType.DMA((2,)),
            pltpu.SemaphoreType.DMA((2,)),
            pltpu.SemaphoreType.REGULAR,
        ],
        compiler_params=pltpu.CompilerParams(
            collective_id=0, has_side_effects=True, vmem_limit_bytes=40 << 20
        ),
    )(pair_input.reshape(4, 8, 32, 128), outgoing_in, outgoing_out, incoming_in, incoming_out)
    return out.reshape(32, 32, 128)


def solution(mesh):
    return jax.shard_map(
        per_device,
        mesh=mesh,
        in_specs=(P("row", "col", None), P(), P(), P(), P()),
        out_specs=P("row", "col", None),
        check_vma=False,
    )
```

```python
import functools

import jax
import jax.numpy as jnp
from jax import lax
from jax.experimental import pallas as pl
from jax.experimental.pallas import tpu as pltpu
from jax.sharding import PartitionSpec as P

MESH = pl.DeviceIdType.MESH
F32 = jnp.float32
BF16 = jnp.bfloat16
EPS = 1e-05


def sigmoid(v):
    return 0.5 * jnp.tanh(0.5 * v) + 0.5


FAR = (2, 1, 3, 0)
RING = (4, 3, 5, 2, 6, 1, 7, 0)


def regroup(tiles):
    lane = lax.broadcasted_iota(jnp.int32, tiles[0].shape, 1)
    low = lane < 64
    even = lane // 32 % 2 == 0
    t = list(tiles)
    for a, b in ((0, 2), (1, 3)):
        t[a], t[b] = (
            jnp.where(low, t[a], pltpu.roll(t[b], 64, 1)),
            jnp.where(low, pltpu.roll(t[a], 64, 1), t[b]),
        )
    for a, b in ((0, 1), (2, 3)):
        t[a], t[b] = (
            jnp.where(even, t[a], pltpu.roll(t[b], 32, 1)),
            jnp.where(even, pltpu.roll(t[a], 96, 1), t[b]),
        )
    return t


def kernel(
    z_hbm, w1_hbm, u1_hbm, w2_hbm, u2_hbm, out_ref,
    z_ref, w1_ref, u1_ref, w2_ref, u2_ref, pair, normed, gate, wt, ut, stage, stage2,
    send, recv, lmat, rmat, tsend, trecv,
    send_sem, recv_sem, ex_send, ex_recv, tsend_sem, trecv_sem, in_sem,
):
    row, col = lax.axis_index("row"), lax.axis_index("col")
    z = lax.rem(row, 8)
    y = lax.div(col, 4)
    x = lax.rem(lax.div(col, 2), 2) * 2 + lax.div(row, 8)
    core = lax.rem(col, 2)
    me = x * 32 + y * 8 + z
    xs = [lax.rem(x + d, 4) for d in range(4)]
    ys = [lax.rem(y + d, 4) for d in range(4)]
    zs = [lax.rem(z + d, 8) for d in range(8)]
    rows = [[lax.rem(a, 2) * 8 + b for b in zs] for a in xs]
    cols = [[b * 4 + lax.div(a, 2) * 2 + core for b in ys] for a in xs]
    sibling = (row, col + 1 - 2 * core)

    inputs = [
        pltpu.make_async_copy(a, b, in_sem.at[n])
        for n, (a, b) in enumerate(
            (
                (z_hbm, z_ref), (w1_hbm, w1_ref), (u1_hbm, u1_ref), (w2_hbm, w2_ref), (u2_hbm, u2_ref),
            )
        )
    ]
    for copy in inputs:
        copy.start()

    barrier = pltpu.get_barrier_semaphore()
    for dx in FAR:
        for dy in FAR:
            for dz in RING:
                if dx or dy or dz:
                    to = (rows[dx][dz], cols[dx][dy])
                    pl.semaphore_signal(barrier, inc=1, device_id=to, device_id_type=MESH)
    pl.semaphore_signal(barrier, inc=1, device_id=sibling, device_id_type=MESH)

    for copy in inputs:
        copy.wait()
    for k, (w_ref, u_ref) in enumerate(((w1_ref, u1_ref), (w2_ref, u2_ref))):
        for b in range(5):
            wt[k, b] = w_ref[:, 128 * b : 128 * b + 128].astype(F32).T.astype(BF16)
        ut[k] = u_ref[...].astype(F32).T.astype(BF16)

    for a in range(8):
        pair[:, 128 * a : 128 * a + 128] = z_ref[:, a].reshape(128, 128).T

    def norm_pair():
        v = pair[...]
        cent = v - jnp.mean(v, axis=0, keepdims=True)
        var = jnp.mean(cent * cent, axis=0, keepdims=True)
        normed[...] = (cent * lax.rsqrt(var + EPS)).astype(BF16)

    def update(k, outgoing):
        norm_pair()
        zn = normed[...]
        if k == 0:
            pl.semaphore_wait(barrier, 128)

        for dx in FAR:
            xd = xs[dx]
            w = wt[k, :4, pl.ds(pl.multiple_of(xd * 32, 32), 32), :].reshape(128, 128)
            p = jnp.dot(w, zn, preferred_element_type=F32)
            left = sigmoid(p[0:32]) * p[32:64]
            right = sigmoid(p[64:96]) * p[96:128]
            for a in range(8):
                stage[pl.ds(a, 32, stride=16), :] = left[:, 128 * a : 128 * a + 128]
                stage[pl.ds(8 + a, 32, stride=16), :] = right[:, 128 * a : 128 * a + 128]
            send[k, xd] = stage[...].reshape(32, 16, 128).astype(BF16)

            if dx == 0:
                recv[k, x, y * 8 + z] = send[k, x, y * 8 + z]
            for dy in FAR:
                for dz in RING:
                    if dx or dy or dz:
                        pltpu.make_async_remote_copy(
                            src_ref=send.at[k, xd, ys[dy] * 8 + zs[dz]],
                            dst_ref=recv.at[k, x, y * 8 + z],
                            send_sem=send_sem.at[k, dx],
                            recv_sem=recv_sem.at[k, dx],
                            device_id=(rows[dx][dz], cols[dx][dy]),
                            device_id_type=MESH,
                        ).start()

        gate[...] = sigmoid(jnp.dot(wt[k, 4], zn, preferred_element_type=F32))

        exchanges = []
        for dx in FAR:
            xo = xs[-dx]
            part = recv.at[k, xo, pl.ds(0, 31)] if dx == 0 else recv.at[k, xo]
            pltpu.make_async_copy(part, part, recv_sem.at[k, dx]).wait()
            kc = lax.div(xo, 2) * 2 + core
            xl = lax.rem(xo, 2)
            for n in range(8):
                tiles = [recv[k, xo, 8 * m + n].astype(F32) for m in range(4)]
                t = regroup(tiles)
                base = n // 2 * 32
                for h in range(2):
                    pair_l = jnp.concatenate([t[2 * h][0:8], t[2 * h + 1][0:8]], axis=0)
                    pair_r = jnp.concatenate([t[2 * h][8:16], t[2 * h + 1][8:16]], axis=0)
                    here = pl.ds(base + 16 * h, 16)
                    lmat[k, kc, xl, n % 2, here, :] = pair_l.astype(BF16)
                    rmat[k, kc, xl, n % 2, here, :] = pair_r.astype(BF16)

            def swap(ref, n):
                copy = pltpu.make_async_remote_copy(
                    src_ref=ref,
                    dst_ref=ref,
                    send_sem=ex_send.at[k, dx, n],
                    recv_sem=ex_recv.at[k, dx, n],
                    device_id=sibling,
                    device_id_type=MESH,
                )
                copy.start()
                exchanges.append(copy)

            swap(lmat.at[k, kc, xl], 0)
            if outgoing:
                swap(rmat.at[k, kc, xl, 1 - core], 1)
        for copy in exchanges:
            copy.wait()

        if outgoing:
            a = jnp.concatenate([lmat[k, kc].reshape(512, 128) for kc in range(4)], axis=1)
            b = jnp.concatenate([rmat[k, kc, :, core].reshape(256, 128) for kc in range(4)], axis=1)
            tri = lax.dot_general(a, b, (((1,), (1,)), ((), ())), preferred_element_type=F32)
        else:
            a = jnp.concatenate([lmat[k, kc].reshape(512, 128) for kc in range(4)], axis=1)
            b = jnp.concatenate([rmat[k, 2 * xh + core].reshape(512, 128) for xh in range(2)], axis=1)
            tri = lax.dot_general(a, b, (((0,), (0,)), ((), ())), preferred_element_type=F32)
        for m in range(16):
            if outgoing:
                r = m // 8 * 8 + m % 4 * 2 + m // 4 % 2
            else:
                r = m % 4 * 4 + m // 4
            for n in range(2):
                tiles = [
                    tri[32 * m + 8 * u : 32 * m + 8 * u + 8, 128 * n : 128 * n + 128]
                    for u in range(4)
                ]
                for t, tile in enumerate(regroup(tiles)):
                    tsend[k, r, 4 * n + t if outgoing else 2 * t + n] = tile.astype(BF16)

        order = [(dx, dy, dz) for dx in FAR for dy in FAR for dz in RING if dx or dy or dz]
        order.sort(key=lambda o: -sum(min(d, n - d) for d, n in zip(o, (4, 4, 8))))
        for dx, dy, dz in order:
            pltpu.make_async_remote_copy(
                src_ref=tsend.at[k, rows[dx][dz], ys[dy] * 2 + lax.div(xs[dx], 2)],
                dst_ref=trecv.at[k, me],
                send_sem=tsend_sem.at[k],
                recv_sem=trecv_sem.at[k],
                device_id=(rows[dx][dz], cols[dx][dy]),
                device_id_type=MESH,
            ).start()
        trecv[k, me] = tsend[k, row, y * 2 + lax.div(x, 2)]
        part = trecv.at[k, pl.ds(0, 127)]
        pltpu.make_async_copy(part, part, trecv_sem.at[k]).wait()

        v = trecv[k].astype(F32)
        cent = v - jnp.mean(v, axis=0, keepdims=True)
        var = jnp.mean(cent * cent, axis=0, keepdims=True)
        stage2[...] = (cent * lax.rsqrt(var + EPS)).reshape(1024, 128)
        tn = jnp.concatenate(
            [stage2[pl.ds(a, 128, stride=8), :].astype(BF16) for a in range(8)], axis=1
        )
        change = jnp.dot(ut[k], tn, preferred_element_type=F32)
        pair[...] = pair[...] + gate[...] * change

    update(0, True)
    update(1, False)

    for a in range(8):
        out_ref[:, a] = pair[:, 128 * a : 128 * a + 128].T.reshape(4, 32, 128)

    for k in range(2):
        for dx in range(4):
            part = send.at[k, 0, pl.ds(0, 31)] if dx == 0 else send.at[k, 0]
            pltpu.make_async_copy(part, part, send_sem.at[k, dx]).wait()
        part = trecv.at[k, pl.ds(0, 127)]
        pltpu.make_async_copy(part, part, tsend_sem.at[k]).wait()


def per_device(pair_input, outgoing_in, outgoing_out, incoming_in, incoming_out):
    vmem = pl.BlockSpec(memory_space=pltpu.VMEM)
    out = pl.pallas_call(
        kernel,
        out_shape=jax.ShapeDtypeStruct((4, 8, 32, 128), F32),
        in_specs=[pl.BlockSpec(memory_space=pltpu.HBM)] * 5,
        out_specs=vmem,
        scratch_shapes=[
            pltpu.VMEM((4, 8, 32, 128), F32),
            pltpu.VMEM((128, 640), BF16),
            pltpu.VMEM((128, 128), BF16),
            pltpu.VMEM((128, 640), BF16),
            pltpu.VMEM((128, 128), BF16),
            pltpu.VMEM((128, 1024), F32),
            pltpu.VMEM((128, 1024), BF16),
            pltpu.VMEM((128, 1024), F32),
            pltpu.VMEM((2, 5, 128, 128), BF16),
            pltpu.VMEM((2, 128, 128), BF16),
            pltpu.VMEM((512, 128), F32),
            pltpu.VMEM((1024, 128), F32),
            pltpu.VMEM((2, 4, 32, 16, 128), BF16),
            pltpu.VMEM((2, 4, 32, 16, 128), BF16),
            pltpu.VMEM((2, 4, 2, 2, 128, 128), BF16),
            pltpu.VMEM((2, 4, 2, 2, 128, 128), BF16),
            pltpu.VMEM((2, 16, 8, 8, 128), BF16),
            pltpu.VMEM((2, 128, 8, 128), BF16),
            pltpu.SemaphoreType.DMA((2, 4)),
            pltpu.SemaphoreType.DMA((2, 4)),
            pltpu.SemaphoreType.DMA((2, 4, 2)),
            pltpu.SemaphoreType.DMA((2, 4, 2)),
            pltpu.SemaphoreType.DMA((2,)),
            pltpu.SemaphoreType.DMA((2,)),
            pltpu.SemaphoreType.DMA((5,)),
        ],
        compiler_params=pltpu.CompilerParams(
            collective_id=0, has_side_effects=True, vmem_limit_bytes=40 << 20
        ),
    )(pair_input.reshape(4, 8, 32, 128), outgoing_in, outgoing_out, incoming_in, incoming_out)
    return out.reshape(32, 32, 128)


def solution(mesh):
    return jax.shard_map(
        per_device,
        mesh=mesh,
        in_specs=(P("row", "col", None), P(), P(), P(), P()),
        out_specs=P("row", "col", None),
        check_vma=False,
    )
```

```python
import functools

import jax
import jax.numpy as jnp
from jax import lax
from jax.experimental import pallas as pl
from jax.experimental.pallas import tpu as pltpu
from jax.sharding import PartitionSpec as P

MESH = pl.DeviceIdType.MESH
F32 = jnp.float32
BF16 = jnp.bfloat16
EPS = 1e-05


def sigmoid(v):
    return 0.5 * jnp.tanh(0.5 * v) + 0.5


FAR = (2, 1, 3, 0)
RING = (4, 3, 5, 2, 6, 1, 7, 0)
OFFSETS = [(dx, dy, dz) for dx in FAR for dy in FAR for dz in RING]
HALF = [(dx, dy, d) for dx in FAR for dy in FAR for d in (2, 1, 3, 0)]
HALF.sort(key=lambda o: -(min(o[0], 4 - o[0]) + min(o[1], 4 - o[1]) + min(2 * o[2], 8 - 2 * o[2])))


def regroup(tiles):
    lane = lax.broadcasted_iota(jnp.int32, tiles[0].shape, 1)
    low = lane < 64
    even = lane // 32 % 2 == 0
    t = list(tiles)
    for a, b in ((0, 2), (1, 3)):
        t[a], t[b] = (
            jnp.where(low, t[a], pltpu.roll(t[b], 64, 1)),
            jnp.where(low, pltpu.roll(t[a], 64, 1), t[b]),
        )
    for a, b in ((0, 1), (2, 3)):
        t[a], t[b] = (
            jnp.where(even, t[a], pltpu.roll(t[b], 32, 1)),
            jnp.where(even, pltpu.roll(t[a], 96, 1), t[b]),
        )
    return t


def kernel(
    z_hbm, w1_hbm, u1_hbm, w2_hbm, u2_hbm, out_ref,
    z_ref, w1_ref, u1_ref, w2_ref, u2_ref, pair, normed, gate, wt, ut, stage, stage2,
    send, recv, lown, lsib, rown, rsib, tsend, trecv,
    send_sem, recv_sem, ex_send, ex_recv, tsend_sem, trecv_sem, in_sem, plane_sem,
):
    row, col = lax.axis_index("row"), lax.axis_index("col")
    z = lax.rem(row, 8)
    y = lax.div(col, 4)
    x = lax.rem(lax.div(col, 2), 2) * 2 + lax.div(row, 8)
    core = lax.rem(col, 2)
    me = x * 32 + y * 8 + z
    xs = [lax.rem(x + d, 4) for d in range(4)]
    ys = [lax.rem(y + d, 4) for d in range(4)]
    zs = [lax.rem(z + d, 8) for d in range(8)]
    rows = [[lax.rem(a, 2) * 8 + b for b in zs] for a in xs]
    cols = [[b * 4 + lax.div(a, 2) * 2 + core for b in ys] for a in xs]
    sibling = (row, col + 1 - 2 * core)

    inputs = [
        pltpu.make_async_copy(a, b, in_sem.at[n])
        for n, (a, b) in enumerate(
            (
                (z_hbm, z_ref), (w1_hbm, w1_ref), (u1_hbm, u1_ref), (w2_hbm, w2_ref), (u2_hbm, u2_ref),
            )
        )
    ]
    for copy in inputs:
        copy.start()

    barrier = pltpu.get_barrier_semaphore()
    for dx, dy, dz in OFFSETS:
        if (dx == 0) != (dy == dz == 0):
            to = (rows[dx][dz], cols[dx][dy])
            pl.semaphore_signal(barrier, inc=1, device_id=to, device_id_type=MESH)
    pl.semaphore_signal(barrier, inc=1, device_id=sibling, device_id_type=MESH)

    for copy in inputs:
        copy.wait()
    for k, (w_ref, u_ref) in enumerate(((w1_ref, u1_ref), (w2_ref, u2_ref))):
        for b in range(5):
            wt[k, b] = w_ref[:, 128 * b : 128 * b + 128].astype(F32).T.astype(BF16)
        ut[k] = u_ref[...].astype(F32).T.astype(BF16)

    for a in range(8):
        pair[:, 128 * a : 128 * a + 128] = z_ref[:, a].reshape(128, 128).T

    def norm_pair():
        v = pair[...]
        cent = v - jnp.mean(v, axis=0, keepdims=True)
        var = jnp.mean(cent * cent, axis=0, keepdims=True)
        normed[...] = (cent * lax.rsqrt(var + EPS)).astype(BF16)

    def update(k, outgoing):
        norm_pair()
        zn = normed[...]
        turns = (0, 2, 1, 3) if k == 0 else FAR

        for dx in turns:
            xd = xs[dx]
            w = wt[k, :4, pl.ds(pl.multiple_of(xd * 32, 32), 32), :].reshape(128, 128)
            p = jnp.dot(w, zn, preferred_element_type=F32)
            left = sigmoid(p[0:32]) * p[32:64]
            right = sigmoid(p[64:96]) * p[96:128]
            for a in range(8):
                stage[pl.ds(a, 32, stride=16), :] = left[:, 128 * a : 128 * a + 128]
                stage[pl.ds(8 + a, 32, stride=16), :] = right[:, 128 * a : 128 * a + 128]
            send[k, xd] = stage[...].reshape(32, 16, 128).astype(BF16)

            if dx == 0:
                recv[k, x, y * 8 + z] = send[k, x, y * 8 + z]
            if k == 0 and dx == 0:
                pl.semaphore_wait(barrier, 35)
                for d in range(1, 4):
                    to = (rows[d][0], cols[d][0])
                    pl.semaphore_signal(plane_sem, inc=1, device_id=to, device_id_type=MESH)
            if k == 0 and dx == turns[1]:
                pl.semaphore_wait(plane_sem, 3)
            for dy in FAR:
                for dz in RING:
                    if dx or dy or dz:
                        pltpu.make_async_remote_copy(
                            src_ref=send.at[k, xd, ys[dy] * 8 + zs[dz]],
                            dst_ref=recv.at[k, x, y * 8 + z],
                            send_sem=send_sem.at[k, dx],
                            recv_sem=recv_sem.at[k, dx],
                            device_id=(rows[dx][dz], cols[dx][dy]),
                            device_id_type=MESH,
                        ).start()

        gate[...] = sigmoid(jnp.dot(wt[k, 4], zn, preferred_element_type=F32))

        exchanges = []
        for dx in turns:
            xo = xs[-dx]
            part = recv.at[k, xo, pl.ds(0, 31)] if dx == 0 else recv.at[k, xo]
            pltpu.make_async_copy(part, part, recv_sem.at[k, dx]).wait()
            xh, xl = lax.div(xo, 2), lax.rem(xo, 2)
            for n in range(8):
                tiles = [recv[k, xo, 8 * m + n].astype(F32) for m in range(4)]
                t = regroup(tiles)
                base = n // 2 * 32
                for h in range(2):
                    pair_l = jnp.concatenate([t[2 * h][0:8], t[2 * h + 1][0:8]], axis=0)
                    pair_r = jnp.concatenate([t[2 * h][8:16], t[2 * h + 1][8:16]], axis=0)
                    here = pl.ds(base + 16 * h, 16)
                    lown[k, xh, xl, n % 2, here, :] = pair_l.astype(BF16)
                    rown[k, xh, xl, n % 2, here, :] = pair_r.astype(BF16)

            def swap(ref, there, n):
                copy = pltpu.make_async_remote_copy(
                    src_ref=ref,
                    dst_ref=there,
                    send_sem=ex_send.at[k, dx, n],
                    recv_sem=ex_recv.at[k, dx, n],
                    device_id=sibling,
                    device_id_type=MESH,
                )
                copy.start()
                exchanges.append(copy)

            swap(lown.at[k, xh, xl], lsib.at[k, xh, xl], 0)
            if outgoing:
                swap(rown.at[k, xh, xl, 1 - core], rsib.at[k, xh, xl, 1 - core], 1)
        for half in range(2):
            parity = core if half == 0 else 1 - core
            if half == (0 if outgoing else 1):
                for copy in exchanges:
                    copy.wait()
            if outgoing:
                a = [m[k, i, :, parity].reshape(256, 128) for m in (lown, lsib) for i in range(2)]
                b = [m[k, i, :, core].reshape(256, 128) for m in (rown, rsib) for i in range(2)]
                dims = (((1,), (1,)), ((), ()))
            else:
                a = [(lown, lsib)[half][k, i].reshape(512, 128) for i in range(2)]
                b = [rown[k, i].reshape(512, 128) for i in range(2)]
                dims = (((0,), (0,)), ((), ()))
            a, b = jnp.concatenate(a, axis=1), jnp.concatenate(b, axis=1)
            tri = lax.dot_general(a, b, dims, preferred_element_type=F32)
            for m in range(8):
                r = m if outgoing else m % 4 * 2 + m // 4
                for n in range(2):
                    tiles = [
                        tri[32 * m + 8 * u : 32 * m + 8 * u + 8, 128 * n : 128 * n + 128]
                        for u in range(4)
                    ]
                    for t, tile in enumerate(regroup(tiles)):
                        tsend[k, half, r, 4 * n + t if outgoing else 2 * t + n] = tile.astype(BF16)

            shift = lax.rem(z + parity, 2)
            for dx, dy, d in HALF:
                zd = lax.rem(z + 2 * d + shift, 8)
                to = lax.rem(xs[dx], 2) * 8 + zd

                def give(half=half, dx=dx, dy=dy, to=to):
                    pltpu.make_async_remote_copy(
                        src_ref=tsend.at[k, half, lax.div(to, 2), ys[dy] * 2 + lax.div(xs[dx], 2)],
                        dst_ref=trecv.at[k, me],
                        send_sem=tsend_sem.at[k],
                        recv_sem=trecv_sem.at[k],
                        device_id=(to, cols[dx][dy]),
                        device_id_type=MESH,
                    ).start()

                if dx or dy or d:
                    give()
                else:
                    pl.when(shift == 1)(give)

                    @pl.when(shift == 0)
                    def _(half=half):
                        trecv[k, me] = tsend[k, half, lax.div(row, 2), y * 2 + lax.div(x, 2)]
        part = trecv.at[k, pl.ds(0, 127)]
        pltpu.make_async_copy(part, part, trecv_sem.at[k]).wait()

        v = trecv[k].astype(F32)
        cent = v - jnp.mean(v, axis=0, keepdims=True)
        var = jnp.mean(cent * cent, axis=0, keepdims=True)
        stage2[...] = (cent * lax.rsqrt(var + EPS)).reshape(1024, 128)
        tn = jnp.concatenate(
            [stage2[pl.ds(a, 128, stride=8), :].astype(BF16) for a in range(8)], axis=1
        )
        change = jnp.dot(ut[k], tn, preferred_element_type=F32)
        pair[...] = pair[...] + gate[...] * change

    update(0, True)
    update(1, False)

    for a in range(8):
        out_ref[:, a] = pair[:, 128 * a : 128 * a + 128].T.reshape(4, 32, 128)

    for k in range(2):
        for dx in range(4):
            part = send.at[k, 0, pl.ds(0, 31)] if dx == 0 else send.at[k, 0]
            pltpu.make_async_copy(part, part, send_sem.at[k, dx]).wait()
        part = trecv.at[k, pl.ds(0, 127)]
        pltpu.make_async_copy(part, part, tsend_sem.at[k]).wait()


def per_device(pair_input, outgoing_in, outgoing_out, incoming_in, incoming_out):
    vmem = pl.BlockSpec(memory_space=pltpu.VMEM)
    out = pl.pallas_call(
        kernel,
        out_shape=jax.ShapeDtypeStruct((4, 8, 32, 128), F32),
        in_specs=[pl.BlockSpec(memory_space=pltpu.HBM)] * 5,
        out_specs=vmem,
        scratch_shapes=[
            pltpu.VMEM((4, 8, 32, 128), F32),
            pltpu.VMEM((128, 640), BF16),
            pltpu.VMEM((128, 128), BF16),
            pltpu.VMEM((128, 640), BF16),
            pltpu.VMEM((128, 128), BF16),
            pltpu.VMEM((128, 1024), F32),
            pltpu.VMEM((128, 1024), BF16),
            pltpu.VMEM((128, 1024), F32),
            pltpu.VMEM((2, 5, 128, 128), BF16),
            pltpu.VMEM((2, 128, 128), BF16),
            pltpu.VMEM((512, 128), F32),
            pltpu.VMEM((1024, 128), F32),
            pltpu.VMEM((2, 4, 32, 16, 128), BF16),
            pltpu.VMEM((2, 4, 32, 16, 128), BF16),
            pltpu.VMEM((2, 2, 2, 2, 128, 128), BF16),
            pltpu.VMEM((2, 2, 2, 2, 128, 128), BF16),
            pltpu.VMEM((2, 2, 2, 2, 128, 128), BF16),
            pltpu.VMEM((2, 2, 2, 2, 128, 128), BF16),
            pltpu.VMEM((2, 2, 8, 8, 8, 128), BF16),
            pltpu.VMEM((2, 128, 8, 128), BF16),
            pltpu.SemaphoreType.DMA((2, 4)),
            pltpu.SemaphoreType.DMA((2, 4)),
            pltpu.SemaphoreType.DMA((2, 4, 2)),
            pltpu.SemaphoreType.DMA((2, 4, 2)),
            pltpu.SemaphoreType.DMA((2,)),
            pltpu.SemaphoreType.DMA((2,)),
            pltpu.SemaphoreType.DMA((5,)),
            pltpu.SemaphoreType.REGULAR,
        ],
        compiler_params=pltpu.CompilerParams(
            collective_id=0, has_side_effects=True, vmem_limit_bytes=40 << 20
        ),
    )(
        *(
            pltpu.with_memory_space_constraint(a, pltpu.HBM)
            for a in (
                pair_input.reshape(4, 8, 32, 128), outgoing_in, outgoing_out, incoming_in, incoming_out,
            )
        )
    )
    return out.reshape(32, 32, 128)


def solution(mesh):
    return jax.shard_map(
        per_device,
        mesh=mesh,
        in_specs=(P("row", "col", None), P(), P(), P(), P()),
        out_specs=P("row", "col", None),
        check_vma=False,
    )
```

```python
import functools

import jax
import jax.numpy as jnp
from jax import lax
from jax.experimental import pallas as pl
from jax.experimental.pallas import tpu as pltpu
from jax.sharding import PartitionSpec as P

MESH = pl.DeviceIdType.MESH
F32 = jnp.float32
BF16 = jnp.bfloat16
EPS = 1e-05


def sigmoid(v):
    return 0.5 * jnp.tanh(0.5 * v) + 0.5


FAR = (2, 1, 3, 0)
RING = (4, 3, 5, 2, 6, 1, 7, 0)
OFFSETS = [(dx, dy, dz) for dx in FAR for dy in FAR for dz in RING]
HALF = [(dx, dy, d) for dx in FAR for dy in FAR for d in (2, 1, 3, 0)]
HALF.sort(key=lambda o: -(min(o[0], 4 - o[0]) + min(o[1], 4 - o[1]) + min(2 * o[2], 8 - 2 * o[2])))


def regroup(tiles):
    lane = lax.broadcasted_iota(jnp.int32, tiles[0].shape, 1)
    low = lane < 64
    even = lane // 32 % 2 == 0
    t = list(tiles)
    for a, b in ((0, 2), (1, 3)):
        t[a], t[b] = (
            jnp.where(low, t[a], pltpu.roll(t[b], 64, 1)),
            jnp.where(low, pltpu.roll(t[a], 64, 1), t[b]),
        )
    for a, b in ((0, 1), (2, 3)):
        t[a], t[b] = (
            jnp.where(even, t[a], pltpu.roll(t[b], 32, 1)),
            jnp.where(even, pltpu.roll(t[a], 96, 1), t[b]),
        )
    return t


def kernel(
    z_hbm, w1_hbm, u1_hbm, w2_hbm, u2_hbm, out_ref,
    z_ref, w1_ref, u1_ref, w2_ref, u2_ref, pair, normed, gate, wt, ut, stage, stage2,
    send, recv, lown, lsib, rown, rsib, tsend, trecv,
    send_sem, recv_sem, ex_send, ex_recv, tsend_sem, trecv_sem, in_sem, plane_sem,
):
    row, col = lax.axis_index("row"), lax.axis_index("col")
    z = lax.rem(row, 8)
    y = lax.div(col, 4)
    x = lax.rem(lax.div(col, 2), 2) * 2 + lax.div(row, 8)
    core = lax.rem(col, 2)
    me = x * 32 + y * 8 + z
    xs = [lax.rem(x + d, 4) for d in range(4)]
    ys = [lax.rem(y + d, 4) for d in range(4)]
    turn = 1 - 2 * lax.rem(x + y, 2)
    zs = [lax.rem(z + 8 + turn * d, 8) for d in range(8)]
    rows = [[lax.rem(a, 2) * 8 + b for b in zs] for a in xs]
    cols = [[b * 4 + lax.div(a, 2) * 2 + core for b in ys] for a in xs]
    sibling = (row, col + 1 - 2 * core)

    inputs = [
        pltpu.make_async_copy(a, b, in_sem.at[n])
        for n, (a, b) in enumerate(
            (
                (z_hbm, z_ref), (w1_hbm, w1_ref), (u1_hbm, u1_ref), (w2_hbm, w2_ref), (u2_hbm, u2_ref),
            )
        )
    ]
    for copy in inputs:
        copy.start()

    barrier = pltpu.get_barrier_semaphore()
    for dx, dy, dz in OFFSETS:
        if (dx == 0) != (dy == dz == 0):
            to = (rows[dx][dz], cols[dx][dy])
            pl.semaphore_signal(barrier, inc=1, device_id=to, device_id_type=MESH)
    pl.semaphore_signal(barrier, inc=1, device_id=sibling, device_id_type=MESH)

    for copy in inputs:
        copy.wait()
    for k, (w_ref, u_ref) in enumerate(((w1_ref, u1_ref), (w2_ref, u2_ref))):
        for b in range(5):
            wt[k, b] = w_ref[:, 128 * b : 128 * b + 128].astype(F32).T.astype(BF16)
        ut[k] = u_ref[...].astype(F32).T.astype(BF16)

    for a in range(8):
        pair[:, 128 * a : 128 * a + 128] = z_ref[:, a].reshape(128, 128).T

    def norm_pair():
        v = pair[...]
        cent = v - jnp.mean(v, axis=0, keepdims=True)
        var = jnp.mean(cent * cent, axis=0, keepdims=True)
        normed[...] = (cent * lax.rsqrt(var + EPS)).astype(BF16)

    def update(k, outgoing):
        norm_pair()
        zn = normed[...]
        turns = (0, 2, 1, 3) if k == 0 else FAR

        for dx in turns:
            xd = xs[dx]
            w = wt[k, :4, pl.ds(pl.multiple_of(xd * 32, 32), 32), :].reshape(128, 128)
            p = jnp.dot(w, zn, preferred_element_type=F32)
            left = sigmoid(p[0:32]) * p[32:64]
            right = sigmoid(p[64:96]) * p[96:128]
            for a in range(8):
                stage[pl.ds(a, 32, stride=16), :] = left[:, 128 * a : 128 * a + 128]
                stage[pl.ds(8 + a, 32, stride=16), :] = right[:, 128 * a : 128 * a + 128]
            send[k, xd] = stage[...].reshape(32, 16, 128).astype(BF16)

            if dx == 0:
                recv[k, x, y * 8 + z] = send[k, x, y * 8 + z]
            if k == 0 and dx == 0:
                pl.semaphore_wait(barrier, 35)
                for d in range(1, 4):
                    to = (rows[d][0], cols[d][0])
                    pl.semaphore_signal(plane_sem, inc=1, device_id=to, device_id_type=MESH)
            if k == 0 and dx == turns[1]:
                pl.semaphore_wait(plane_sem, 3)
            for dz in RING:
                for dy in FAR:
                    if dx or dy or dz:
                        pltpu.make_async_remote_copy(
                            src_ref=send.at[k, xd, ys[dy] * 8 + zs[dz]],
                            dst_ref=recv.at[k, x, y * 8 + z],
                            send_sem=send_sem.at[k, dx],
                            recv_sem=recv_sem.at[k, dx],
                            device_id=(rows[dx][dz], cols[dx][dy]),
                            device_id_type=MESH,
                        ).start()

        gate[...] = sigmoid(jnp.dot(wt[k, 4], zn, preferred_element_type=F32))

        exchanges = []
        for dx in turns:
            xo = xs[-dx]
            part = recv.at[k, xo, pl.ds(0, 31)] if dx == 0 else recv.at[k, xo]
            pltpu.make_async_copy(part, part, recv_sem.at[k, dx]).wait()
            xh, xl = lax.div(xo, 2), lax.rem(xo, 2)
            for n in range(8):
                tiles = [recv[k, xo, 8 * m + n].astype(F32) for m in range(4)]
                t = regroup(tiles)
                base = n // 2 * 32
                for h in range(2):
                    pair_l = jnp.concatenate([t[2 * h][0:8], t[2 * h + 1][0:8]], axis=0)
                    pair_r = jnp.concatenate([t[2 * h][8:16], t[2 * h + 1][8:16]], axis=0)
                    here = pl.ds(base + 16 * h, 16)
                    lown[k, xh, xl, n % 2, here, :] = pair_l.astype(BF16)
                    rown[k, xh, xl, n % 2, here, :] = pair_r.astype(BF16)

            def swap(ref, there, n):
                copy = pltpu.make_async_remote_copy(
                    src_ref=ref,
                    dst_ref=there,
                    send_sem=ex_send.at[k, dx, n],
                    recv_sem=ex_recv.at[k, dx, n],
                    device_id=sibling,
                    device_id_type=MESH,
                )
                copy.start()
                exchanges.append(copy)

            swap(lown.at[k, xh, xl], lsib.at[k, xh, xl], 0)
            if outgoing:
                swap(rown.at[k, xh, xl, 1 - core], rsib.at[k, xh, xl, 1 - core], 1)
        for half in range(2):
            parity = core if half == 0 else 1 - core
            if half == (0 if outgoing else 1):
                for copy in exchanges:
                    copy.wait()
            if outgoing:
                a = [m[k, i, :, parity].reshape(256, 128) for m in (lown, lsib) for i in range(2)]
                b = [m[k, i, :, core].reshape(256, 128) for m in (rown, rsib) for i in range(2)]
                dims = (((1,), (1,)), ((), ()))
            else:
                a = [(lown, lsib)[half][k, i].reshape(512, 128) for i in range(2)]
                b = [rown[k, i].reshape(512, 128) for i in range(2)]
                dims = (((0,), (0,)), ((), ()))
            a, b = jnp.concatenate(a, axis=1), jnp.concatenate(b, axis=1)
            tri = lax.dot_general(a, b, dims, preferred_element_type=F32)
            for m in range(8):
                r = m if outgoing else m % 4 * 2 + m // 4
                for n in range(2):
                    tiles = [
                        tri[32 * m + 8 * u : 32 * m + 8 * u + 8, 128 * n : 128 * n + 128]
                        for u in range(4)
                    ]
                    for t, tile in enumerate(regroup(tiles)):
                        tsend[k, half, r, 4 * n + t if outgoing else 2 * t + n] = tile.astype(BF16)

            shift = lax.rem(z + parity, 2)
            for dx, dy, d in HALF:
                zd = lax.rem(z + 2 * d + shift, 8)
                to = lax.rem(xs[dx], 2) * 8 + zd

                def give(half=half, dx=dx, dy=dy, to=to):
                    pltpu.make_async_remote_copy(
                        src_ref=tsend.at[k, half, lax.div(to, 2), ys[dy] * 2 + lax.div(xs[dx], 2)],
                        dst_ref=trecv.at[k, me],
                        send_sem=tsend_sem.at[k],
                        recv_sem=trecv_sem.at[k],
                        device_id=(to, cols[dx][dy]),
                        device_id_type=MESH,
                    ).start()

                if dx or dy or d:
                    give()
                else:
                    pl.when(shift == 1)(give)

                    @pl.when(shift == 0)
                    def _(half=half):
                        trecv[k, me] = tsend[k, half, lax.div(row, 2), y * 2 + lax.div(x, 2)]
        part = trecv.at[k, pl.ds(0, 127)]
        pltpu.make_async_copy(part, part, trecv_sem.at[k]).wait()

        v = trecv[k].astype(F32)
        cent = v - jnp.mean(v, axis=0, keepdims=True)
        var = jnp.mean(cent * cent, axis=0, keepdims=True)
        stage2[...] = (cent * lax.rsqrt(var + EPS)).reshape(1024, 128)
        tn = jnp.concatenate(
            [stage2[pl.ds(a, 128, stride=8), :].astype(BF16) for a in range(8)], axis=1
        )
        change = jnp.dot(ut[k], tn, preferred_element_type=F32)
        pair[...] = pair[...] + gate[...] * change

    update(0, True)
    update(1, False)

    for a in range(8):
        out_ref[:, a] = pair[:, 128 * a : 128 * a + 128].T.reshape(4, 32, 128)

    for k in range(2):
        for dx in range(4):
            part = send.at[k, 0, pl.ds(0, 31)] if dx == 0 else send.at[k, 0]
            pltpu.make_async_copy(part, part, send_sem.at[k, dx]).wait()
        part = trecv.at[k, pl.ds(0, 127)]
        pltpu.make_async_copy(part, part, tsend_sem.at[k]).wait()


def per_device(pair_input, outgoing_in, outgoing_out, incoming_in, incoming_out):
    vmem = pl.BlockSpec(memory_space=pltpu.VMEM)
    out = pl.pallas_call(
        kernel,
        out_shape=jax.ShapeDtypeStruct((4, 8, 32, 128), F32),
        in_specs=[pl.BlockSpec(memory_space=pltpu.HBM)] * 5,
        out_specs=vmem,
        scratch_shapes=[
            pltpu.VMEM((4, 8, 32, 128), F32),
            pltpu.VMEM((128, 640), BF16),
            pltpu.VMEM((128, 128), BF16),
            pltpu.VMEM((128, 640), BF16),
            pltpu.VMEM((128, 128), BF16),
            pltpu.VMEM((128, 1024), F32),
            pltpu.VMEM((128, 1024), BF16),
            pltpu.VMEM((128, 1024), F32),
            pltpu.VMEM((2, 5, 128, 128), BF16),
            pltpu.VMEM((2, 128, 128), BF16),
            pltpu.VMEM((512, 128), F32),
            pltpu.VMEM((1024, 128), F32),
            pltpu.VMEM((2, 4, 32, 16, 128), BF16),
            pltpu.VMEM((2, 4, 32, 16, 128), BF16),
            pltpu.VMEM((2, 2, 2, 2, 128, 128), BF16),
            pltpu.VMEM((2, 2, 2, 2, 128, 128), BF16),
            pltpu.VMEM((2, 2, 2, 2, 128, 128), BF16),
            pltpu.VMEM((2, 2, 2, 2, 128, 128), BF16),
            pltpu.VMEM((2, 2, 8, 8, 8, 128), BF16),
            pltpu.VMEM((2, 128, 8, 128), BF16),
            pltpu.SemaphoreType.DMA((2, 4)),
            pltpu.SemaphoreType.DMA((2, 4)),
            pltpu.SemaphoreType.DMA((2, 4, 2)),
            pltpu.SemaphoreType.DMA((2, 4, 2)),
            pltpu.SemaphoreType.DMA((2,)),
            pltpu.SemaphoreType.DMA((2,)),
            pltpu.SemaphoreType.DMA((5,)),
            pltpu.SemaphoreType.REGULAR,
        ],
        compiler_params=pltpu.CompilerParams(
            collective_id=0, has_side_effects=True, vmem_limit_bytes=40 << 20
        ),
    )(
        *(
            pltpu.with_memory_space_constraint(a, pltpu.HBM)
            for a in (
                pair_input.reshape(4, 8, 32, 128), outgoing_in, outgoing_out, incoming_in, incoming_out,
            )
        )
    )
    return out.reshape(32, 32, 128)


def solution(mesh):
    return jax.shard_map(
        per_device,
        mesh=mesh,
        in_specs=(P("row", "col", None), P(), P(), P(), P()),
        out_specs=P("row", "col", None),
        check_vma=False,
    )
```

```python
import functools

import jax
import jax.numpy as jnp
from jax import lax
from jax.experimental import pallas as pl
from jax.experimental.pallas import tpu as pltpu
from jax.sharding import PartitionSpec as P

MESH = pl.DeviceIdType.MESH
F32 = jnp.float32
BF16 = jnp.bfloat16
EPS = 1e-05


def sigmoid(v):
    return 0.5 * jnp.tanh(0.5 * v) + 0.5


FAR = (2, 1, 3, 0)
RING = (4, 3, 5, 2, 6, 1, 7, 0)
OFFSETS = [(dx, dy, dz) for dx in FAR for dy in FAR for dz in RING]
HALF = [(dx, dy, d) for dx in FAR for dy in FAR for d in (2, 1, 3, 0)]
HALF.sort(key=lambda o: -(min(o[0], 4 - o[0]) + min(o[1], 4 - o[1]) + min(2 * o[2] + 0.5, 7.5 - 2 * o[2])))


def regroup(tiles):
    lane = lax.broadcasted_iota(jnp.int32, tiles[0].shape, 1)
    low = lane < 64
    even = lane // 32 % 2 == 0
    t = list(tiles)
    for a, b in ((0, 2), (1, 3)):
        t[a], t[b] = (
            jnp.where(low, t[a], pltpu.roll(t[b], 64, 1)),
            jnp.where(low, pltpu.roll(t[a], 64, 1), t[b]),
        )
    for a, b in ((0, 1), (2, 3)):
        t[a], t[b] = (
            jnp.where(even, t[a], pltpu.roll(t[b], 32, 1)),
            jnp.where(even, pltpu.roll(t[a], 96, 1), t[b]),
        )
    return t


def kernel(
    z_hbm, w1_hbm, u1_hbm, w2_hbm, u2_hbm, out_ref,
    z_ref, w1_ref, u1_ref, w2_ref, u2_ref, pair, normed, gate, wt, ut, gate_rows, pair_rows, stage, stage2,
    send, recv, lown, lsib, rown, rsib, tsend, trecv,
    send_sem, recv_sem, ex_send, ex_recv, tsend_sem, trecv_sem, in_sem, plane_sem,
):
    row, col = lax.axis_index("row"), lax.axis_index("col")
    z = lax.rem(row, 8)
    y = lax.div(col, 4)
    x = lax.rem(lax.div(col, 2), 2) * 2 + lax.div(row, 8)
    core = lax.rem(col, 2)
    me = x * 32 + y * 8 + z
    xs = [lax.rem(x + d, 4) for d in range(4)]
    ys = [lax.rem(y + d, 4) for d in range(4)]
    turn = 1 - 2 * lax.rem(x + y, 2)
    zs = [lax.rem(z + 8 + turn * d, 8) for d in range(8)]
    rows = [[lax.rem(a, 2) * 8 + b for b in zs] for a in xs]
    cols = [[b * 4 + lax.div(a, 2) * 2 + core for b in ys] for a in xs]
    sibling = (row, col + 1 - 2 * core)

    inputs = [
        pltpu.make_async_copy(a, b, in_sem.at[n])
        for n, (a, b) in enumerate(
            (
                (z_hbm, z_ref), (w1_hbm, w1_ref), (u1_hbm, u1_ref), (w2_hbm, w2_ref), (u2_hbm, u2_ref),
            )
        )
    ]
    barrier = pltpu.get_barrier_semaphore()
    for dx, dy, dz in OFFSETS:
        if (dx == 0) != (dy == dz == 0):
            to = (rows[dx][dz], cols[dx][dy])
            pl.semaphore_signal(barrier, inc=1, device_id=to, device_id_type=MESH)
    pl.semaphore_signal(barrier, inc=1, device_id=sibling, device_id_type=MESH)

    for copy in inputs:
        copy.start()
    for copy in inputs:
        copy.wait()
    for k, (w_ref, u_ref) in enumerate(((w1_ref, u1_ref), (w2_ref, u2_ref))):
        for b in range(5):
            wt[k, b] = w_ref[:, 128 * b : 128 * b + 128].astype(F32).T.astype(BF16)
        ut[k] = u_ref[...].astype(F32).T.astype(BF16)

    for a in range(8):
        pair[:, 128 * a : 128 * a + 128] = z_ref[:, a].reshape(128, 128).T

    def norm_pair():
        v = pair[...]
        cent = v - jnp.mean(v, axis=0, keepdims=True)
        var = jnp.mean(cent * cent, axis=0, keepdims=True)
        normed[...] = (cent * lax.rsqrt(var + EPS)).astype(BF16)

    def update(k, outgoing):
        norm_pair()
        zn = normed[...]
        turns = (0, 2, 1, 3) if k == 0 else FAR

        for dx in turns:
            xd = xs[dx]
            w = wt[k, :4, pl.ds(pl.multiple_of(xd * 32, 32), 32), :].reshape(128, 128)
            p = jnp.dot(w, zn, preferred_element_type=F32)
            left = sigmoid(p[0:32]) * p[32:64]
            right = sigmoid(p[64:96]) * p[96:128]
            for a in range(8):
                stage[pl.ds(a, 32, stride=16), :] = left[:, 128 * a : 128 * a + 128]
                stage[pl.ds(8 + a, 32, stride=16), :] = right[:, 128 * a : 128 * a + 128]
            send[k, xd] = stage[...].reshape(32, 16, 128).astype(BF16)

            if dx == 0:
                recv[k, x, y * 8 + z] = send[k, x, y * 8 + z]
            if k == 0 and dx == 0:
                pl.semaphore_wait(barrier, 35)
                for d in range(1, 4):
                    to = (rows[d][0], cols[d][0])
                    pl.semaphore_signal(plane_sem, inc=1, device_id=to, device_id_type=MESH)
            if k == 0 and dx == turns[1]:
                pl.semaphore_wait(plane_sem, 3)
            for dz in RING:
                for dy in FAR:
                    if dx or dy or dz:
                        pltpu.make_async_remote_copy(
                            src_ref=send.at[k, xd, ys[dy] * 8 + zs[dz]],
                            dst_ref=recv.at[k, x, y * 8 + z],
                            send_sem=send_sem.at[k, dx],
                            recv_sem=recv_sem.at[k, dx],
                            device_id=(rows[dx][dz], cols[dx][dy]),
                            device_id_type=MESH,
                        ).start()

        gate[...] = sigmoid(jnp.dot(wt[k, 4], zn, preferred_element_type=F32))
        if k == 1:
            for a in range(8):
                gate_rows[a] = gate[:, 128 * a : 128 * a + 128].T
                pair_rows[a] = pair[:, 128 * a : 128 * a + 128].T

        exchanges = []
        for dx in turns:
            xo = xs[-dx]
            part = recv.at[k, xo, pl.ds(0, 31)] if dx == 0 else recv.at[k, xo]
            pltpu.make_async_copy(part, part, recv_sem.at[k, dx]).wait()
            xh, xl = lax.div(xo, 2), lax.rem(xo, 2)
            for n in range(8):
                tiles = [recv[k, xo, 8 * m + n].astype(F32) for m in range(4)]
                t = regroup(tiles)
                base = n // 2 * 32
                for h in range(2):
                    pair_l = jnp.concatenate([t[2 * h][0:8], t[2 * h + 1][0:8]], axis=0)
                    pair_r = jnp.concatenate([t[2 * h][8:16], t[2 * h + 1][8:16]], axis=0)
                    here = pl.ds(base + 16 * h, 16)
                    lown[k, xh, xl, n % 2, here, :] = pair_l.astype(BF16)
                    rown[k, xh, xl, n % 2, here, :] = pair_r.astype(BF16)

            def swap(ref, there, n):
                copy = pltpu.make_async_remote_copy(
                    src_ref=ref,
                    dst_ref=there,
                    send_sem=ex_send.at[k, dx, n],
                    recv_sem=ex_recv.at[k, dx, n],
                    device_id=sibling,
                    device_id_type=MESH,
                )
                copy.start()
                exchanges.append(copy)

            swap(lown.at[k, xh, xl], lsib.at[k, xh, xl], 0)
            if outgoing:
                swap(rown.at[k, xh, xl, 1 - core], rsib.at[k, xh, xl, 1 - core], 1)
        def over_own_columns(lm, rm, parity):
            a = jnp.concatenate([lm[k, i, :, parity].reshape(256, 128) for i in range(2)], axis=1)
            b = jnp.concatenate([rm[k, i, :, core].reshape(256, 128) for i in range(2)], axis=1)
            return lax.dot_general(a, b, (((1,), (1,)), ((), ())), preferred_element_type=F32)

        if outgoing:
            mine = [over_own_columns(lown, rown, p) for p in (core, 1 - core)]
        for half in range(2):
            parity = core if half == 0 else 1 - core
            if half == (0 if outgoing else 1):
                for copy in exchanges:
                    copy.wait()
            if outgoing:
                tri = mine[half] + over_own_columns(lsib, rsib, parity)
            else:
                a = jnp.concatenate([(lown, lsib)[half][k, i].reshape(512, 128) for i in range(2)], axis=1)
                b = jnp.concatenate([rown[k, i].reshape(512, 128) for i in range(2)], axis=1)
                tri = lax.dot_general(a, b, (((0,), (0,)), ((), ())), preferred_element_type=F32)
            for m in range(8):
                r = m if outgoing else m % 4 * 2 + m // 4
                for n in range(2):
                    tiles = [
                        tri[32 * m + 8 * u : 32 * m + 8 * u + 8, 128 * n : 128 * n + 128]
                        for u in range(4)
                    ]
                    for t, tile in enumerate(regroup(tiles)):
                        tsend[k, half, r, 4 * n + t if outgoing else 2 * t + n] = tile.astype(BF16)

            shift = lax.rem(z + parity, 2)
            for dx, dy, d in HALF:
                zd = lax.rem(z + 8 + turn * (2 * d + shift), 8)
                to = lax.rem(xs[dx], 2) * 8 + zd

                def give(half=half, dx=dx, dy=dy, to=to):
                    pltpu.make_async_remote_copy(
                        src_ref=tsend.at[k, half, lax.div(to, 2), ys[dy] * 2 + lax.div(xs[dx], 2)],
                        dst_ref=trecv.at[k, me],
                        send_sem=tsend_sem.at[k],
                        recv_sem=trecv_sem.at[k],
                        device_id=(to, cols[dx][dy]),
                        device_id_type=MESH,
                    ).start()

                if dx or dy or d:
                    give()
                else:
                    pl.when(shift == 1)(give)

                    @pl.when(shift == 0)
                    def _(half=half):
                        trecv[k, me] = tsend[k, half, lax.div(row, 2), y * 2 + lax.div(x, 2)]
        part = trecv.at[k, pl.ds(0, 127)]
        pltpu.make_async_copy(part, part, trecv_sem.at[k]).wait()

        v = trecv[k].astype(F32)
        cent = v - jnp.mean(v, axis=0, keepdims=True)
        var = jnp.mean(cent * cent, axis=0, keepdims=True)
        stage2[...] = (cent * lax.rsqrt(var + EPS)).reshape(1024, 128)
        if k == 1:
            for a in range(8):
                tn = stage2[pl.ds(a, 128, stride=8), :].T.astype(BF16)
                change = jnp.dot(tn, u2_ref[...], preferred_element_type=F32)
                out_ref[:, a] = (pair_rows[a] + gate_rows[a] * change).reshape(4, 32, 128)
            return
        tn = jnp.concatenate(
            [stage2[pl.ds(a, 128, stride=8), :].astype(BF16) for a in range(8)], axis=1
        )
        change = jnp.dot(ut[k], tn, preferred_element_type=F32)
        pair[...] = pair[...] + gate[...] * change

    update(0, True)
    update(1, False)

    for k in range(2):
        for dx in range(4):
            part = send.at[k, 0, pl.ds(0, 31)] if dx == 0 else send.at[k, 0]
            pltpu.make_async_copy(part, part, send_sem.at[k, dx]).wait()
        part = trecv.at[k, pl.ds(0, 127)]
        pltpu.make_async_copy(part, part, tsend_sem.at[k]).wait()


def per_device(pair_input, outgoing_in, outgoing_out, incoming_in, incoming_out):
    vmem = pl.BlockSpec(memory_space=pltpu.VMEM)
    out = pl.pallas_call(
        kernel,
        out_shape=jax.ShapeDtypeStruct((4, 8, 32, 128), F32),
        in_specs=[pl.BlockSpec(memory_space=pltpu.HBM)] * 5,
        out_specs=vmem,
        scratch_shapes=[
            pltpu.VMEM((4, 8, 32, 128), F32),
            pltpu.VMEM((128, 640), BF16),
            pltpu.VMEM((128, 128), BF16),
            pltpu.VMEM((128, 640), BF16),
            pltpu.VMEM((128, 128), BF16),
            pltpu.VMEM((128, 1024), F32),
            pltpu.VMEM((128, 1024), BF16),
            pltpu.VMEM((128, 1024), F32),
            pltpu.VMEM((2, 5, 128, 128), BF16),
            pltpu.VMEM((2, 128, 128), BF16),
            pltpu.VMEM((8, 128, 128), F32),
            pltpu.VMEM((8, 128, 128), F32),
            pltpu.VMEM((512, 128), F32),
            pltpu.VMEM((1024, 128), F32),
            pltpu.VMEM((2, 4, 32, 16, 128), BF16),
            pltpu.VMEM((2, 4, 32, 16, 128), BF16),
            pltpu.VMEM((2, 2, 2, 2, 128, 128), BF16),
            pltpu.VMEM((2, 2, 2, 2, 128, 128), BF16),
            pltpu.VMEM((2, 2, 2, 2, 128, 128), BF16),
            pltpu.VMEM((2, 2, 2, 2, 128, 128), BF16),
            pltpu.VMEM((2, 2, 8, 8, 8, 128), BF16),
            pltpu.VMEM((2, 128, 8, 128), BF16),
            pltpu.SemaphoreType.DMA((2, 4)),
            pltpu.SemaphoreType.DMA((2, 4)),
            pltpu.SemaphoreType.DMA((2, 4, 2)),
            pltpu.SemaphoreType.DMA((2, 4, 2)),
            pltpu.SemaphoreType.DMA((2,)),
            pltpu.SemaphoreType.DMA((2,)),
            pltpu.SemaphoreType.DMA((5,)),
            pltpu.SemaphoreType.REGULAR,
        ],
        compiler_params=pltpu.CompilerParams(
            collective_id=0, has_side_effects=True, vmem_limit_bytes=40 << 20
        ),
    )(
        *(
            pltpu.with_memory_space_constraint(a, pltpu.HBM)
            for a in (
                pair_input.reshape(4, 8, 32, 128), outgoing_in, outgoing_out, incoming_in, incoming_out,
            )
        )
    )
    return out.reshape(32, 32, 128)


def solution(mesh):
    return jax.shard_map(
        per_device,
        mesh=mesh,
        in_specs=(P("row", "col", None), P(), P(), P(), P()),
        out_specs=P("row", "col", None),
        check_vma=False,
    )
```
